128 devices in a mesh: seq: 8 (over x, core), head: 16 (over z, y).
Axes of the slice: x: 4, y: 4, z: 4, core: 2. Of those that a mesh axis runs over, the one named last changes fastest.
Arguments:
- queries: bfloat16 [32768, 2048], P(('seq', 'head')), may hold values from -9 to 9
- keys: bfloat16 [32768, 2048], P(('seq', 'head')), may hold values from -9 to 9
- values: bfloat16 [32768, 2048], P(('seq', 'head')), may hold values from -6 to 6
Outputs:
- attended: bfloat16 [32768, 2048], P(('seq', 'head'))
The draws below stay inside these ranges and needn't reach their ends.
All inputs are finite; a program needn't handle non-finite values.
Results may differ from the reference program's by a relative error of at most 0.0038.
Values may be sent and summed in bfloat16 or wider, within the bound.
A program may use at most 128 MiB of HBM per device.

```python
import jax
import jax.numpy as jnp
from jax import lax

H = 16
HD = 128
SEG = 2048
LEVELS = 5
TOKENS = 32768


def draw_queries(key, part):
    key = jax.random.fold_in(key, 101)
    field = jax.random.truncated_normal(key, -6.0, 6.0, (TOKENS, H * HD), jnp.float32)
    return field.astype(jnp.bfloat16)


def draw_keys(key, part):
    key = jax.random.fold_in(key, 202)
    field = jax.random.truncated_normal(key, -6.0, 6.0, (TOKENS, H * HD), jnp.float32)
    return field.astype(jnp.bfloat16)


def block_levels(own_key, shape, pieces, least, high):
    def one(dim, blocks):
        draws = jax.random.uniform(jax.random.fold_in(jax.random.fold_in(own_key, 6), dim), (blocks,), jnp.float32, least / len(pieces), high / len(pieces))
        return jnp.repeat(jnp.exp(draws), shape[dim] // blocks).reshape((-1,) + (1,) * (len(shape) - dim - 1))

    gain = one(*pieces[0])
    for cut in pieces[1:]:
        gain = gain * one(*cut)
    return gain


def bell_draw(own_key, shape, spread, reach, cuts=(), kind=jnp.bfloat16):
    drawn = jax.random.normal(own_key, shape, jnp.float32) * spread
    if len(cuts) > 0:
        drawn = block_levels(own_key, shape, cuts, -0.22, 0.18) * drawn
    return jnp.clip(drawn, min=-reach, max=reach).astype(kind)


def setup_inputs(seed: int = 0) -> dict:
    streams_of = jax.random.split(jax.random.key(seed), 4)
    return {
        "queries": draw_queries(jax.random.fold_in(streams_of[3], 71), 0),
        "keys": draw_keys(jax.random.fold_in(streams_of[3], 71), 0),
        "values": bell_draw(streams_of[2], (TOKENS, H * HD), 1.0, 6.0, ((0, 128),)),
    }


def attend_rows(query_rows, key_rows, value_rows, query_start):
    factor = query_rows.shape[-1] ** -0.5
    scores = jnp.dot(query_rows, key_rows.T, preferred_element_type=jnp.float32) * factor
    query_pos = query_start + jnp.arange(query_rows.shape[0], dtype=jnp.int32)
    key_pos = jnp.arange(key_rows.shape[0], dtype=jnp.int32)
    visible = key_pos[None, :] <= query_pos[:, None]
    scores = jnp.where(visible, scores, -jnp.inf)
    row_top = jnp.max(scores, axis=1)
    expo_terms = jnp.exp(scores - row_top[:, None])
    row_total = jnp.sum(expo_terms, axis=1)
    weights = expo_terms.astype(jnp.bfloat16)
    partial_out = jnp.dot(weights, value_rows, preferred_element_type=jnp.float32)
    return partial_out, row_total, row_top


def attend_packed(packed):
    return attend_rows(packed[0], packed[1], packed[2], 0)


def dilate(source, seg_rows, stride, offset):
    segments = source.shape[0] // (seg_rows * stride)
    shaped = source.reshape(segments, seg_rows, stride, source.shape[1])
    return lax.dynamic_index_in_dim(shaped, offset, 2, keepdims=False)


def initial_state(length, columns):
    return (jnp.full((length,), -jnp.inf, jnp.float32), jnp.zeros((length,), jnp.float32), jnp.zeros((length, columns), jnp.float32))


def merge_level(carry_state, stride, offset, partial_out, row_total, row_top):
    old_top, old_total, old_acc = carry_state
    length = old_top.shape[0]
    columns = old_acc.shape[1]
    top_view = old_top.reshape(length // stride, stride)
    total_view = old_total.reshape(length // stride, stride)
    acc_view = old_acc.reshape(length // stride, stride, columns)
    top_here = lax.dynamic_index_in_dim(top_view, offset, 1, keepdims=False)
    total_here = lax.dynamic_index_in_dim(total_view, offset, 1, keepdims=False)
    acc_here = lax.dynamic_index_in_dim(acc_view, offset, 1, keepdims=False)
    new_top = jnp.maximum(top_here, row_top)
    keep_old = jnp.exp(top_here - new_top)
    keep_new = jnp.exp(row_top - new_top)
    new_total = total_here * keep_old + row_total * keep_new
    new_acc = acc_here * keep_old[:, None] + partial_out * keep_new[:, None]
    top_view = lax.dynamic_update_index_in_dim(top_view, new_top[:, None], offset, 1)
    total_view = lax.dynamic_update_index_in_dim(total_view, new_total[:, None], offset, 1)
    acc_view = lax.dynamic_update_index_in_dim(acc_view, new_acc[:, None, :], offset, 1)
    return (top_view.reshape(length), total_view.reshape(length), acc_view.reshape(length, columns))


def finish_state(carry_state):
    return (carry_state[2] / carry_state[1][:, None]).astype(jnp.bfloat16)


def reference(queries, keys, values):
    head_outputs = []
    for head_index in range(H):
        lo_col = head_index * HD
        q_head = queries[:, lo_col:lo_col + HD]
        k_head = keys[:, lo_col:lo_col + HD]
        v_head = values[:, lo_col:lo_col + HD]
        carry_state = initial_state(TOKENS, HD)
        for level_index in range(LEVELS):
            stride = 2 ** level_index
            offset = head_index % stride
            query_rows = dilate(q_head, SEG, stride, offset)
            key_rows = dilate(k_head, SEG, stride, offset)
            value_rows = dilate(v_head, SEG, stride, offset)
            partial_out, row_total, row_top = lax.map(attend_packed, (query_rows, key_rows, value_rows))
            carry_state = merge_level(carry_state, stride, offset, partial_out.reshape(-1, HD), row_total.reshape(-1), row_top.reshape(-1))
        head_outputs.append(finish_state(carry_state))
    return jnp.concatenate(head_outputs, axis=1)
```

```python
import functools
import math

import jax
import jax.numpy as jnp
from jax import lax
from jax.experimental import pallas as pl
from jax.experimental.pallas import tpu as pltpu
from jax.sharding import PartitionSpec as P

HD = 128
BLK = 256
NB = 16
CH = 64
NCH = BLK // CH
SCALE = HD**-0.5 * math.log2(math.e)
LOW = -1e30
MESH = pl.DeviceIdType.MESH

ORDER = [
    (0, 1), (0, 3), (1, 0), (3, 0),
    (1, 1), (3, 3), (1, 3), (3, 1),
    (2, 2), (0, 2), (2, 0),
    (1, 2), (3, 2), (2, 1), (2, 3),
]

KV_PARTS = [(0, 64), (64, 128), (128, 256)]
Q_PARTS = [(i * CH, (i + 1) * CH) for i in range(NCH)]


def token_of(row, head):
    group = row // 16
    shift = jnp.where(
        group >= 8,
        1 + (group - 8) * 2,
        jnp.where(
            group >= 4,
            2 + (group - 4) * 4,
            jnp.where(group >= 2, 4 + (group - 2) * 8, jnp.where(group >= 1, 8, 0)),
        ),
    )
    return (row % 16) * 16 + (shift + head) % 16


def class_of(row):
    return (
        (row < 128).astype(jnp.int32)
        + (row < 64).astype(jnp.int32)
        + (row < 32).astype(jnp.int32)
        + (row < 16).astype(jnp.int32)
    )


def iota(shape, dim):
    return lax.broadcasted_iota(jnp.int32, shape, dim)


def kernel(
    q_hbm, k_hbm, v_hbm, out_ref,
    x_in, q_send, k_send, v_send, q_recv, k_recv, v_recv, o_send, o_recv,
    kx2, vx2, kx3, vx3, kx4, vx4,
    m_ref, acc_ref, bias_ref, mult0, mult1, mult2, mult3,
    in_sem, q_ss, k_ss, v_ss, o_ss, q_rs, k_rs, v_rs, o_rs, x_ss, x_rs,
):
    seq = lax.axis_index("seq")
    me = lax.axis_index("head")
    z, y = me // 4, me % 4
    flip = 1 + 2 * (seq % 2)
    peers = [((z + dz * flip) % 4) * 4 + (y + dy * flip) % 4 for dz, dy in ORDER]

    loads = []
    for i, src in enumerate((k_hbm, v_hbm, q_hbm)):
        cp = pltpu.make_async_copy(src, x_in.at[i], in_sem.at[i])
        cp.start()
        loads.append(cp)

    barrier = pltpu.get_barrier_semaphore()
    for p in peers:
        pl.semaphore_signal(barrier, inc=1, device_id=(seq, p), device_id_type=MESH)
    for d in range(1, 8):
        pl.semaphore_signal(
            barrier, inc=1, device_id=((seq + d) % 8, me), device_id_type=MESH
        )

    def sort_rows(i, dst):
        def body(j, carry):
            tok = token_of(iota((BLK, BLK), 0), j)
            perm = (iota((BLK, BLK), 1) == tok).astype(jnp.bfloat16)
            cols = x_in[i, :, pl.ds(pl.multiple_of(j * HD, HD), HD)]
            dst[j] = jnp.dot(perm, cols, preferred_element_type=jnp.float32).astype(
                jnp.bfloat16
            )
            return carry

        lax.fori_loop(0, NB, body, 0)

    def send(src, dst, ssem, rsem, part, idx):
        lo, hi = part
        rows = pl.ds(lo, hi - lo)
        for p in peers:
            pltpu.make_async_remote_copy(
                src_ref=src.at[p, rows],
                dst_ref=dst.at[me, rows],
                send_sem=ssem.at[idx],
                recv_sem=rsem.at[idx],
                device_id=(seq, p),
                device_id_type=MESH,
            ).start()

    def wait_all(buf, sem, part, idx):
        lo, hi = part
        view = buf.at[pl.ds(0, NB - 1), pl.ds(lo, hi - lo)]
        pltpu.make_async_copy(view, view, sem.at[idx]).wait()

    loads[0].wait()
    sort_rows(0, k_send)
    k_recv[me] = k_send[me]
    pl.semaphore_wait(barrier, NB - 1 + 7)
    send(k_send, k_recv, k_ss, k_rs, KV_PARTS[0], 0)
    loads[1].wait()
    sort_rows(1, v_send)
    v_recv[me] = v_send[me]
    send(v_send, v_recv, v_ss, v_rs, KV_PARTS[0], 0)
    loads[2].wait()
    sort_rows(2, q_send)
    q_recv[me] = q_send[me]
    send(q_send, q_recv, q_ss, q_rs, Q_PARTS[0], 0)
    for i in range(1, len(KV_PARTS)):
        send(k_send, k_recv, k_ss, k_rs, KV_PARTS[i], i)
        send(v_send, v_recv, v_ss, v_rs, KV_PARTS[i], i)
    for i in range(1, NCH):
        send(q_send, q_recv, q_ss, q_rs, Q_PARTS[i], i)

    row_tok = token_of(iota((BLK, BLK), 0), me)
    col_tok = token_of(iota((BLK, BLK), 1), me)
    bias_ref[...] = jnp.where(col_tok <= row_tok, 0.0, LOW)
    for ref, period, level in ((mult0, 128, 0), (mult1, 128, 1), (mult2, 64, 2), (mult3, 32, 3)):
        shape = ref.shape
        both = jnp.minimum(
            class_of(iota(shape, 0)), class_of(iota(shape, 1) % period)
        )
        ref[...] = (1 + both - level).astype(jnp.float32)
    m_ref[...] = jnp.full(m_ref.shape, LOW, jnp.float32)
    acc_ref[...] = jnp.zeros(acc_ref.shape, jnp.float32)

    wait_all(k_recv, k_rs, KV_PARTS[0], 0)
    wait_all(v_recv, v_rs, KV_PARTS[0], 0)

    def hop(src, dst, idx, target):
        return pltpu.make_async_remote_copy(
            src_ref=src,
            dst_ref=dst,
            send_sem=x_ss.at[idx],
            recv_sem=x_rs.at[idx],
            device_id=(target, me),
            device_id_type=MESH,
        )

    @pl.when(seq < 4)
    def _():
        for t in range(4, 8):
            hop(k_recv.at[:, pl.ds(0, 16)], kx4.at[seq % 4], 4, t).start()
            hop(v_recv.at[:, pl.ds(0, 16)], vx4.at[seq % 4], 5, t).start()

    @pl.when(seq % 4 < 2)
    def _():
        for t in range(2, 4):
            hop(k_recv.at[:, pl.ds(0, 32)], kx3.at[seq % 2], 2, (seq // 4) * 4 + t).start()
            hop(v_recv.at[:, pl.ds(0, 32)], vx3.at[seq % 2], 3, (seq // 4) * 4 + t).start()

    @pl.when(seq % 2 == 0)
    def _():
        hop(k_recv.at[:, pl.ds(0, 64)], kx2, 0, (seq // 2) * 2 + 1).start()
        hop(v_recv.at[:, pl.ds(0, 64)], vx2, 1, (seq // 2) * 2 + 1).start()

    def flash(chunk, blk0, nblk, rows, keys, vals, mask=False, mults=(), first=False):
        lo, hi = rows
        height = hi - lo
        length = nblk * height
        blocks = pl.ds(blk0, nblk)
        q = q_recv[blocks, pl.ds(chunk * CH + lo, height)].reshape(length, HD)
        s = lax.dot_general(
            q, keys, (((1,), (1,)), ((), ())), preferred_element_type=jnp.float32
        )
        if mask:
            s0 = s[:height] + bias_ref[pl.ds(chunk * CH + lo, height)]
            s = s0 if nblk == 1 else jnp.concatenate([s0, s[height:]], axis=0)
        width = keys.shape[0]
        lanes = [s[:, i : i + HD] for i in range(0, width, HD)]
        top = functools.reduce(jnp.maximum, lanes)
        top = jnp.broadcast_to(jnp.max(top, axis=1, keepdims=True), (length, HD))
        here = pl.ds(lo, height)
        if not first:
            old = m_ref[blocks, here].reshape(length, HD)
            top = jnp.maximum(old, top)
            keep = jnp.exp2((old - top) * SCALE)
        m_ref[blocks, here] = top.reshape(nblk, height, HD)
        weights = []
        for i, part in enumerate(lanes):
            w = jnp.exp2((part - top) * SCALE)
            if i < len(mults) and mults[i] is not None:
                w = (w.reshape(nblk, height, HD) * mults[i][None]).reshape(length, HD)
            weights.append(w.astype(jnp.bfloat16))
        w = jnp.concatenate(weights, axis=1)
        ones = jnp.ones((width, HD), jnp.bfloat16)
        pv = jnp.dot(
            w, jnp.concatenate([vals, ones], axis=1), preferred_element_type=jnp.float32
        )
        if not first:
            old_acc = acc_ref[blocks, here].reshape(length, 2 * HD)
            pv = pv + old_acc * jnp.concatenate([keep, keep], axis=1)
        acc_ref[blocks, here] = pv.reshape(nblk, height, 2 * HD)

    def cross(chunk, blk0, nblk, rows, key_at, val_at, mult):
        def body(j, carry):
            flash(chunk, blk0, nblk, rows, key_at(j), val_at(j), mults=[mult] * 4)
            return carry

        lax.fori_loop(0, 2, body, 0)

    wait_all(q_recv, q_rs, Q_PARTS[0], 0)

    @pl.when(seq % 2 == 1)
    def _():
        hop(kx2, kx2, 0, seq).wait_recv()
        hop(vx2, vx2, 1, seq).wait_recv()
        for g in range(2):
            cross(
                0, g * 8, 8, (0, 64),
                lambda j: kx2[pl.ds(j * 8, 8)].reshape(512, HD),
                lambda j: vx2[pl.ds(j * 8, 8)].reshape(512, HD),
                mult2[...],
            )

    @pl.when(seq % 4 >= 2)
    def _():
        hop(kx3, kx3, 2, seq).wait_recv()
        hop(vx3, vx3, 3, seq).wait_recv()
        cross(
            0, 0, NB, (0, 32),
            lambda j: kx3[j].reshape(512, HD),
            lambda j: vx3[j].reshape(512, HD),
            mult3[...],
        )

    @pl.when(seq >= 4)
    def _():
        hop(kx4, kx4, 4, seq).wait_recv()
        hop(vx4, vx4, 5, seq).wait_recv()
        cross(
            0, 0, NB, (0, 16),
            lambda j: kx4[pl.ds(j * 2, 2)].reshape(512, HD),
            lambda j: vx4[pl.ds(j * 2, 2)].reshape(512, HD),
            None,
        )

    for i in range(1, len(KV_PARTS)):
        wait_all(k_recv, k_rs, KV_PARTS[i], i)
        wait_all(v_recv, v_rs, KV_PARTS[i], i)

    for chunk in range(NCH):
        if chunk > 0:
            wait_all(q_recv, q_rs, Q_PARTS[chunk], chunk)
        lo = chunk * CH
        nested = lo < 128

        def segment(g, carry, chunk=chunk, lo=lo, nested=nested):
            for kb in range(8):
                flash(
                    chunk, g * 8 + kb, 8 - kb, (0, CH),
                    k_recv[g * 8 + kb], v_recv[g * 8 + kb],
                    mask=True,
                    mults=[mult0[pl.ds(lo, CH)]] if nested else (),
                    first=chunk > 0 and kb == 0,
                )
            return carry

        lax.fori_loop(0, 2, segment, 0)
        if nested:
            cross(
                chunk, 8, 8, (0, CH),
                lambda j: k_recv[pl.ds(j * 4, 4), pl.ds(0, 128)].reshape(512, HD),
                lambda j: v_recv[pl.ds(j * 4, 4), pl.ds(0, 128)].reshape(512, HD),
                mult1[...] if chunk == 0 else None,
            )
        for b in range(NB):
            acc = acc_ref[b]
            o_send[b, pl.ds(lo, CH)] = (acc[:, :HD] / acc[:, HD:]).astype(jnp.bfloat16)
        o_recv[me, pl.ds(lo, CH)] = o_send[me, pl.ds(lo, CH)]
        send(o_send, o_recv, o_ss, o_rs, Q_PARTS[chunk], chunk)

    for i in range(NCH):
        wait_all(o_recv, o_rs, Q_PARTS[i], i)

    def unsort(j, carry):
        tok = token_of(iota((BLK, BLK), 1), j)
        perm = (iota((BLK, BLK), 0) == tok).astype(jnp.bfloat16)
        out_ref[:, pl.ds(pl.multiple_of(j * HD, HD), HD)] = jnp.dot(
            perm, o_recv[j], preferred_element_type=jnp.float32
        ).astype(jnp.bfloat16)
        return carry

    lax.fori_loop(0, NB, unsort, 0)

    for i, part in enumerate(KV_PARTS):
        wait_all(k_send, k_ss, part, i)
        wait_all(v_send, v_ss, part, i)
    for i, part in enumerate(Q_PARTS):
        wait_all(q_send, q_ss, part, i)
        wait_all(o_send, o_ss, part, i)

    @pl.when(seq < 4)
    def _():
        hop(kx4, kx4, 4, seq).wait_send()
        hop(vx4, vx4, 5, seq).wait_send()

    @pl.when(seq % 4 < 2)
    def _():
        hop(kx3, kx3, 2, seq).wait_send()
        hop(vx3, vx3, 3, seq).wait_send()

    @pl.when(seq % 2 == 0)
    def _():
        hop(kx2, kx2, 0, seq).wait_send()
        hop(vx2, vx2, 1, seq).wait_send()


def shards(queries, keys, values):
    bf, f32 = jnp.bfloat16, jnp.float32
    vm = pltpu.VMEM
    blocks = vm((NB, BLK, HD), bf)
    dma = pltpu.SemaphoreType.DMA
    nkv = len(KV_PARTS)
    return pl.pallas_call(
        kernel,
        out_shape=jax.ShapeDtypeStruct((BLK, NB * HD), bf),
        in_specs=[pl.BlockSpec(memory_space=pl.ANY)] * 3,
        out_specs=pl.BlockSpec(memory_space=pltpu.VMEM),
        scratch_shapes=[
            vm((3, BLK, NB * HD), bf),
            *[blocks] * 8,
            vm((NB, 64, HD), bf), vm((NB, 64, HD), bf),
            vm((2, NB, 32, HD), bf), vm((2, NB, 32, HD), bf),
            vm((4, NB, 16, HD), bf), vm((4, NB, 16, HD), bf),
            vm((NB, CH, HD), f32), vm((NB, CH, 2 * HD), f32),
            vm((BLK, BLK), f32), vm((128, 128), f32), vm((64, 128), f32),
            vm((64, 128), f32), vm((32, 128), f32),
            dma((3,)), dma((NCH,)), dma((nkv,)), dma((nkv,)), dma((NCH,)),
            dma((NCH,)), dma((nkv,)), dma((nkv,)), dma((NCH,)), dma((6,)), dma((6,)),
        ],
        compiler_params=pltpu.CompilerParams(
            collective_id=0, has_side_effects=True, vmem_limit_bytes=56 * 2**20
        ),
    )(queries, keys, values)


def solution(mesh):
    spec = P(("seq", "head"), None)
    return jax.shard_map(
        shards, mesh=mesh, in_specs=(spec, spec, spec), out_specs=spec, check_vma=False
    )
```

```python
import functools
import math

import jax
import jax.numpy as jnp
from jax import lax
from jax.experimental import pallas as pl
from jax.experimental.pallas import tpu as pltpu
from jax.sharding import PartitionSpec as P

HD = 128
BLK = 256
NB = 16
CH = 64
NCH = BLK // CH
FAR_AFTER = 2
SCALE = HD**-0.5 * math.log2(math.e)
LOW = -1e30
MESH = pl.DeviceIdType.MESH

ORDER = [
    (1, 2), (3, 2), (2, 1), (2, 3),
    (0, 1), (0, 3), (1, 0), (3, 0),
    (2, 2), (1, 1), (3, 3),
    (0, 2), (2, 0), (1, 3), (3, 1),
]

K_PARTS = [(0, 64), (64, 256)]
Q_PARTS = [(i * CH, (i + 1) * CH) for i in range(NCH)]


SHIFTS = [0, 8, 4, 12, 2, 6, 10, 14, 1, 3, 5, 7, 9, 11, 13, 15]


def token_of(row, head):
    group = row >> 4
    shift = jnp.where(
        group >= 8,
        1 + ((group - 8) << 1),
        jnp.where(
            group >= 4,
            2 + ((group - 4) << 2),
            jnp.where(group >= 2, 4 + ((group - 2) << 3), jnp.where(group >= 1, 8, 0)),
        ),
    )
    return ((row & 15) << 4) + ((shift + head) & 15)


def class_of(row):
    return (
        (row < 128).astype(jnp.int32)
        + (row < 64).astype(jnp.int32)
        + (row < 32).astype(jnp.int32)
        + (row < 16).astype(jnp.int32)
    )


def iota(shape, dim):
    return lax.broadcasted_iota(jnp.int32, shape, dim)


def kernel(
    q_hbm, k_hbm, v_hbm, o_recv,
    x_in, q_send, k_send, v_raw, q_recv, k_recv, v_recv, o_send,
    kx2, vx2, kx3, vx3, kx4, vx4,
    m_ref, l_ref, acc_ref, perm_ref, own_perm, bias_ref, mult0, mult1, mult2, mult3,
    in_sem, own_sem, q_ss, k_ss, v_ss, o_ss, q_rs, k_rs, v_rs, o_rs, x_ss, x_rs,
):
    seq = lax.axis_index("seq")
    me = lax.axis_index("head")
    z, y = me // 4, me % 4
    flip = 1 + 2 * (seq % 2)
    peers = [((z + dz * flip) % 4) * 4 + (y + dy * flip) % 4 for dz, dy in ORDER]

    loads = []
    for i, src in enumerate((k_hbm, q_hbm)):
        cp = pltpu.make_async_copy(src, x_in.at[i], in_sem.at[i])
        cp.start()
        loads.append(cp)

    barrier = pltpu.get_barrier_semaphore()
    for p in peers:
        pl.semaphore_signal(barrier, inc=1, device_id=(seq, p), device_id_type=MESH)
    for d in range(1, 8):
        pl.semaphore_signal(
            barrier, inc=1, device_id=((seq + d) % 8, me), device_id_type=MESH
        )

    rows = iota((BLK, BLK), 0)
    perm_ref[...] = (iota((BLK, BLK), 1) == ((rows & 15) << 4) + (rows >> 4)).astype(
        jnp.bfloat16
    )

    def sort_rows(i, dst):
        for j in range(0, NB, 2):
            pair = jnp.dot(
                perm_ref[...],
                x_in[i, :, j * HD : (j + 2) * HD],
                preferred_element_type=jnp.float32,
            ).astype(jnp.bfloat16)
            for h in (j, j + 1):
                cols = pair[:, (h - j) * HD : (h - j + 1) * HD]
                for g, shift in enumerate(SHIFTS):
                    r = (h + shift) % 16
                    dst[h, g * 16 : (g + 1) * 16] = cols[r * 16 : (r + 1) * 16]

    def send(src, dst, ssem, rsem, part, idx, between=()):
        lo, hi = part
        rows = pl.ds(lo, hi - lo)
        for i, p in enumerate(peers):
            pltpu.make_async_remote_copy(
                src_ref=src.at[p, rows],
                dst_ref=dst.at[me, rows],
                send_sem=ssem.at[idx],
                recv_sem=rsem.at[idx],
                device_id=(seq, p),
                device_id_type=MESH,
            ).start()
            if i < len(between):
                between[i]()

    def wait_all(buf, sem, part, idx):
        lo, hi = part
        view = buf.at[pl.ds(0, NB - 1), pl.ds(lo, hi - lo)]
        pltpu.make_async_copy(view, view, sem.at[idx]).wait()

    def head_cols(ref, h):
        return ref.at[:, pl.ds(pl.multiple_of(h * HD, HD), HD)]

    own = pltpu.make_async_copy(head_cols(v_hbm, me), v_raw.at[me], own_sem)
    own.start()
    pl.semaphore_wait(barrier, NB - 1 + 7)
    for p in peers:
        pltpu.make_async_remote_copy(
            src_ref=head_cols(v_hbm, p),
            dst_ref=v_raw.at[me],
            send_sem=v_ss,
            recv_sem=v_rs,
            device_id=(seq, p),
            device_id_type=MESH,
        ).start()
    loads[0].wait()
    sort_rows(0, k_send)
    send(k_send, k_recv, k_ss, k_rs, K_PARTS[0], 0)
    loads[1].wait()
    sort_rows(1, q_send)
    send(q_send, q_recv, q_ss, q_rs, Q_PARTS[0], 0)
    send(k_send, k_recv, k_ss, k_rs, K_PARTS[1], 1)
    k_recv[me] = k_send[me]
    q_recv[me] = q_send[me]

    row_tok = token_of(iota((BLK, BLK), 0), me)
    col_tok = token_of(iota((BLK, BLK), 1), me)
    own_perm[...] = (iota((BLK, BLK), 1) == row_tok).astype(jnp.bfloat16)
    bias_ref[...] = jnp.where(col_tok <= row_tok, 0.0, LOW)
    for ref, period, level in ((mult0, 128, 0), (mult1, 128, 1), (mult2, 64, 2), (mult3, 32, 3)):
        shape = ref.shape
        both = jnp.minimum(
            class_of(iota(shape, 0)), class_of(iota(shape, 1) & (period - 1))
        )
        ref[...] = (1 + both - level).astype(jnp.float32)

    m_ref[0] = jnp.full(m_ref.shape[1:], LOW, jnp.float32)
    l_ref[0] = jnp.zeros(l_ref.shape[1:], jnp.float32)
    acc_ref[0] = jnp.zeros(acc_ref.shape[1:], jnp.float32)

    own.wait()
    arrived = v_raw.at[pl.ds(0, NB - 1)]
    pltpu.make_async_copy(arrived, arrived, v_rs).wait()
    for b in range(0, NB, 2):
        pair = jnp.dot(
            own_perm[...],
            jnp.concatenate([v_raw[b], v_raw[b + 1]], axis=1),
            preferred_element_type=jnp.float32,
        ).astype(jnp.bfloat16)
        v_recv[b] = pair[:, :HD]
        v_recv[b + 1] = pair[:, HD:]
    wait_all(k_recv, k_rs, K_PARTS[0], 0)

    def hop(src, dst, idx, target):
        return pltpu.make_async_remote_copy(
            src_ref=src,
            dst_ref=dst,
            send_sem=x_ss.at[idx],
            recv_sem=x_rs.at[idx],
            device_id=(target, me),
            device_id_type=MESH,
        )

    @pl.when(seq % 2 == 0)
    def _():
        hop(k_recv.at[:, pl.ds(0, 64)], kx2, 0, (seq // 2) * 2 + 1).start()
        hop(v_recv.at[:, pl.ds(0, 64)], vx2, 1, (seq // 2) * 2 + 1).start()

    core = seq % 2
    partner = seq + 1 - 2 * core
    near_chip = seq % 4 < 2
    far_chip = seq < 4

    def hop3(src, dst, idx):
        @pl.when(near_chip)
        def _():
            hop(src.at[:, pl.ds(0, 32)], dst.at[core], idx, (seq + 2) % 8).start()

    def hop4(src, dst, idx, step):
        @pl.when(far_chip)
        def _():
            target = 4 + 2 * step + core
            hop(src.at[:, pl.ds(0, 16)], dst.at[core, seq // 2 % 2], idx, target).start()

    hops = [functools.partial(hop3, *x) for x in ((k_recv, kx3, 2), (v_recv, vx3, 3))]
    hops += [
        functools.partial(hop4, *x, step)
        for step in range(2)
        for x in ((k_recv, kx4, 4), (v_recv, vx4, 5))
    ]
    send(q_send, q_recv, q_ss, q_rs, Q_PARTS[1], 1, between=hops)
    for i in range(2, NCH):
        send(q_send, q_recv, q_ss, q_rs, Q_PARTS[i], i)

    def hand_over():
        for here, pairs in (
            (jnp.logical_not(near_chip), ((kx3, 2), (vx3, 3))),
            (jnp.logical_not(far_chip), ((kx4, 4), (vx4, 5))),
        ):

            @pl.when(here)
            def _(pairs=pairs):
                for buf, idx in pairs:
                    hop(buf.at[core], buf.at[core], idx, partner).wait_recv()
                    hop(buf.at[core], buf.at[core], idx + 4, partner).start()

    def flash(chunk, blk0, nblk, rows, keys, vals, mask=False, mults=(), first=False):
        lo, hi = rows
        height = hi - lo
        length = nblk * height
        blocks = pl.ds(blk0, nblk)
        q = q_recv[blocks, pl.ds(chunk * CH + lo, height)].reshape(length, HD)
        s = lax.dot_general(
            q, keys, (((1,), (1,)), ((), ())), preferred_element_type=jnp.float32
        )
        if mask:
            s0 = s[:height] + bias_ref[pl.ds(chunk * CH + lo, height)]
            s = s0 if nblk == 1 else jnp.concatenate([s0, s[height:]], axis=0)
        width = keys.shape[0]
        lanes = [s[:, i : i + HD] for i in range(0, width, HD)]
        top = functools.reduce(jnp.maximum, lanes)
        top = jnp.broadcast_to(jnp.max(top, axis=1, keepdims=True), (length, HD))
        here = pl.ds(lo, height)
        state = min(chunk, 1)
        if not first:
            old = m_ref[state, blocks, here].reshape(length, HD)
            top = jnp.maximum(old, top)
            keep = jnp.exp2((old - top) * SCALE)
        m_ref[state, blocks, here] = top.reshape(nblk, height, HD)
        weights = []
        total = jnp.zeros((length, HD), jnp.float32)
        for i, part in enumerate(lanes):
            w = jnp.exp2((part - top) * SCALE)
            if i < len(mults) and mults[i] is not None:
                w = (w.reshape(nblk, height, HD) * mults[i][None]).reshape(length, HD)
            total = total + w
            weights.append(w.astype(jnp.bfloat16))
        pv = jnp.dot(
            jnp.concatenate(weights, axis=1), vals, preferred_element_type=jnp.float32
        )
        if not first:
            pv = pv + acc_ref[state, blocks, here].reshape(length, HD) * keep
            total = total + l_ref[state, blocks, here].reshape(length, HD) * keep
        acc_ref[state, blocks, here] = pv.reshape(nblk, height, HD)
        l_ref[state, blocks, here] = total.reshape(nblk, height, HD)

    def cross(chunk, blk0, nblk, rows, key_at, val_at, mult):
        for j in range(2):
            flash(chunk, blk0, nblk, rows, key_at(j), val_at(j), mults=[mult] * 4)

    wait_all(q_recv, q_rs, Q_PARTS[0], 0)

    @pl.when(seq % 2 == 1)
    def _():
        hop(kx2, kx2, 0, seq).wait_recv()
        hop(vx2, vx2, 1, seq).wait_recv()
        for g in range(2):
            cross(
                0, g * 8, 8, (0, 64),
                lambda j: kx2[pl.ds(j * 8, 8)].reshape(512, HD),
                lambda j: vx2[pl.ds(j * 8, 8)].reshape(512, HD),
                mult2[...],
            )

    def far_rows():
        @pl.when(seq % 4 >= 2)
        def _():
            hop(kx3.at[1 - core], kx3.at[1 - core], 6, partner).wait_recv()
            hop(vx3.at[1 - core], vx3.at[1 - core], 7, partner).wait_recv()
            cross(
                0, 0, NB, (0, 32),
                lambda j: kx3[j].reshape(512, HD),
                lambda j: vx3[j].reshape(512, HD),
                mult3[...],
            )

        @pl.when(seq >= 4)
        def _():
            hop(kx4.at[1 - core], kx4.at[1 - core], 8, partner).wait_recv()
            hop(vx4.at[1 - core], vx4.at[1 - core], 9, partner).wait_recv()
            cross(
                0, 0, NB, (0, 16),
                lambda j: kx4[j].reshape(512, HD),
                lambda j: vx4[j].reshape(512, HD),
                None,
            )

    wait_all(k_recv, k_rs, K_PARTS[1], 1)

    def own_rows(chunk):
        lo = chunk * CH
        nested = lo < 128

        def segment(g, carry):
            for kb in range(8):
                flash(
                    chunk, g * 8 + kb, 8 - kb, (0, CH),
                    k_recv[g * 8 + kb], v_recv[g * 8 + kb],
                    mask=True,
                    mults=[mult0[pl.ds(lo, CH)]] if nested else (),
                    first=chunk > 0 and kb == 0,
                )
            return carry

        segment(0, 0)
        segment(1, 0)
        if nested:
            cross(
                chunk, 8, 8, (0, CH),
                lambda j: k_recv[pl.ds(j * 4, 4), pl.ds(0, 128)].reshape(512, HD),
                lambda j: v_recv[pl.ds(j * 4, 4), pl.ds(0, 128)].reshape(512, HD),
                mult1[...] if chunk == 0 else None,
            )

    def finish(chunk):
        lo = chunk * CH
        state = min(chunk, 1)
        for b in range(NB):
            total = jnp.sum(l_ref[state, b], axis=1, keepdims=True)
            o_send[b, pl.ds(lo, CH)] = (acc_ref[state, b] / total).astype(jnp.bfloat16)
        o_recv[me, pl.ds(lo, CH)] = o_send[me, pl.ds(lo, CH)]
        send(o_send, o_recv, o_ss, o_rs, Q_PARTS[chunk], chunk)

    own_rows(0)
    for chunk in range(1, NCH):
        wait_all(q_recv, q_rs, Q_PARTS[chunk], chunk)
        own_rows(chunk)
        finish(chunk)
        if chunk == 1:
            hand_over()
        if chunk == FAR_AFTER:
            far_rows()
            finish(0)

    for i in range(NCH):
        wait_all(o_recv, o_rs, Q_PARTS[i], i)

    pltpu.make_async_copy(arrived, arrived, v_ss).wait()
    for i, part in enumerate(K_PARTS):
        wait_all(k_send, k_ss, part, i)
    for i, part in enumerate(Q_PARTS):
        wait_all(q_send, q_ss, part, i)
        wait_all(o_send, o_ss, part, i)

    for first, here, bufs in (
        (2, near_chip, (kx3.at[0], vx3.at[0])),
        (6, jnp.logical_not(near_chip), (kx3.at[0], vx3.at[0])),
        (4, far_chip, (kx4.at[0], vx4.at[0])),
        (8, jnp.logical_not(far_chip), (kx4.at[0], vx4.at[0])),
    ):

        @pl.when(here)
        def _(first=first, bufs=bufs):
            for i, buf in enumerate(bufs):
                hop(buf, buf, first + i, partner).wait_send()

    @pl.when(seq % 2 == 0)
    def _():
        hop(kx2, kx2, 0, seq).wait_send()
        hop(vx2, vx2, 1, seq).wait_send()


def unsort_kernel(o_ref, out_hbm, stage, sems):
    rows = iota((BLK, BLK), 0)
    perm = (iota((BLK, BLK), 1) == ((rows & 15) << 4) + (rows >> 4)).astype(jnp.bfloat16)
    copies = []
    for j in range(0, NB, 2):
        cols = []
        for h in (j, j + 1):
            groups = [SHIFTS.index((r - h) % 16) for r in range(16)]
            cols.append(
                jnp.concatenate([o_ref[h, g * 16 : (g + 1) * 16] for g in groups], axis=0)
            )
        stage[:, j * HD : (j + 2) * HD] = jnp.dot(
            perm, jnp.concatenate(cols, axis=1), preferred_element_type=jnp.float32
        ).astype(jnp.bfloat16)
        if j % 4 == 2:
            here = (slice(None), pl.ds((j - 2) * HD, 4 * HD))
            copy = pltpu.make_async_copy(stage.at[here], out_hbm.at[here], sems.at[j // 4])
            copy.start()
            copies.append(copy)
    for copy in copies:
        copy.wait()


def shards(queries, keys, values):
    bf, f32 = jnp.bfloat16, jnp.float32
    vm = pltpu.VMEM
    blocks = vm((NB, BLK, HD), bf)
    dma = pltpu.SemaphoreType.DMA
    nk = len(K_PARTS)
    queries, keys, values = (
        pltpu.with_memory_space_constraint(x, pltpu.HBM) for x in (queries, keys, values)
    )
    sorted_out = pl.pallas_call(
        kernel,
        out_shape=pltpu.VMEM((NB, BLK, HD), bf),
        in_specs=[pl.BlockSpec(memory_space=pltpu.HBM)] * 3,
        out_specs=pl.BlockSpec(memory_space=pltpu.VMEM),
        scratch_shapes=[
            vm((2, BLK, NB * HD), bf),
            *[blocks] * 7,
            vm((NB, 64, HD), bf), vm((NB, 64, HD), bf),
            vm((2, NB, 32, HD), bf), vm((2, NB, 32, HD), bf),
            vm((2, 2, NB, 16, HD), bf), vm((2, 2, NB, 16, HD), bf),
            *[vm((2, NB, CH, HD), f32)] * 3,
            vm((BLK, BLK), bf), vm((BLK, BLK), bf), vm((BLK, BLK), f32),
            vm((128, 128), f32), vm((64, 128), f32), vm((64, 128), f32), vm((32, 128), f32),
            dma((2,)), dma, dma((NCH,)), dma((nk,)), dma, dma((NCH,)),
            dma((NCH,)), dma((nk,)), dma, dma((NCH,)), dma((10,)), dma((10,)),
        ],
        compiler_params=pltpu.CompilerParams(
            collective_id=0, has_side_effects=True, vmem_limit_bytes=48 * 2**20
        ),
    )(queries, keys, values)
    sorted_out = pltpu.with_memory_space_constraint(sorted_out, pltpu.VMEM)
    return pl.pallas_call(
        unsort_kernel,
        out_shape=jax.ShapeDtypeStruct((BLK, NB * HD), bf),
        in_specs=[pl.BlockSpec(memory_space=pltpu.VMEM)],
        out_specs=pl.BlockSpec(memory_space=pl.ANY),
        scratch_shapes=[vm((BLK, NB * HD), bf), dma((4,))],
        compiler_params=pltpu.CompilerParams(vmem_limit_bytes=16 * 2**20),
    )(sorted_out)


def solution(mesh):
    spec = P(("seq", "head"), None)
    return jax.shard_map(
        shards, mesh=mesh, in_specs=(spec, spec, spec), out_specs=spec, check_vma=False
    )
```

```python
import functools
import math

import jax
import jax.numpy as jnp
from jax import lax
from jax.experimental import pallas as pl
from jax.experimental.pallas import tpu as pltpu
from jax.sharding import PartitionSpec as P

HD = 128
BLK = 256
NB = 16
CH = 64
NCH = BLK // CH
FAR_AFTER = 2
SCALE = HD**-0.5 * math.log2(math.e)
LOW = -1e30
MESH = pl.DeviceIdType.MESH

ORDER = [
    (1, 2), (3, 2), (2, 1), (2, 3),
    (0, 1), (0, 3), (1, 0), (3, 0),
    (2, 2), (1, 1), (3, 3),
    (0, 2), (2, 0), (1, 3), (3, 1),
]

K_PARTS = [(0, 64), (64, 256)]
Q_PARTS = [(i * CH, (i + 1) * CH) for i in range(NCH)]


SHIFTS = [0, 8, 4, 12, 2, 6, 10, 14, 1, 3, 5, 7, 9, 11, 13, 15]


def token_of(row, head):
    group = row >> 4
    shift = jnp.where(
        group >= 8,
        1 + ((group - 8) << 1),
        jnp.where(
            group >= 4,
            2 + ((group - 4) << 2),
            jnp.where(group >= 2, 4 + ((group - 2) << 3), jnp.where(group >= 1, 8, 0)),
        ),
    )
    return ((row & 15) << 4) + ((shift + head) & 15)


def class_of(row):
    return (
        (row < 128).astype(jnp.int32)
        + (row < 64).astype(jnp.int32)
        + (row < 32).astype(jnp.int32)
        + (row < 16).astype(jnp.int32)
    )


def iota(shape, dim):
    return lax.broadcasted_iota(jnp.int32, shape, dim)


def kernel(
    q_hbm, k_hbm, v_hbm, o_recv,
    x_in, q_send, k_send, v_raw, q_recv, k_recv, v_recv, o_send,
    kx2, vx2, kx3, vx3, kx4, vx4,
    m_ref, l_ref, acc_ref, perm_ref, own_perm, bias_ref, mult0, mult1, mult2, mult3,
    in_sem, own_sem, q_ss, k_ss, v_ss, o_ss, q_rs, k_rs, v_rs, o_rs, x_ss, x_rs,
):
    seq = lax.axis_index("seq")
    me = lax.axis_index("head")
    z, y = me // 4, me % 4
    flip = 1 + 2 * (seq % 2)
    peers = [((z + dz * flip) % 4) * 4 + (y + dy * flip) % 4 for dz, dy in ORDER]

    barrier = pltpu.get_barrier_semaphore()
    for p in peers:
        pl.semaphore_signal(barrier, inc=1, device_id=(seq, p), device_id_type=MESH)
    core = seq % 2
    partner = seq + 1 - 2 * core
    other_half = (seq // 4 + 1) % 2 * 4 + core
    beside = seq + 2 - 4 * (seq // 2 % 2)
    for t in (partner, beside, other_half, other_half + 2):
        pl.semaphore_signal(barrier, inc=1, device_id=(t, me), device_id_type=MESH)

    loads = []
    for i, src in enumerate((k_hbm, q_hbm)):
        cp = pltpu.make_async_copy(src, x_in.at[i], in_sem.at[i])
        cp.start()
        loads.append(cp)

    def sort_rows(i, dst):
        for j in range(0, NB, 2):
            pair = jnp.dot(
                perm_ref[...],
                x_in[i, :, j * HD : (j + 2) * HD],
                preferred_element_type=jnp.float32,
            ).astype(jnp.bfloat16)
            for h in (j, j + 1):
                cols = pair[:, (h - j) * HD : (h - j + 1) * HD]
                for g, shift in enumerate(SHIFTS):
                    r = (h + shift) % 16
                    dst[h, g * 16 : (g + 1) * 16] = cols[r * 16 : (r + 1) * 16]

    def send(src, dst, ssem, rsem, part, idx, between=()):
        lo, hi = part
        rows = pl.ds(lo, hi - lo)
        for i, p in enumerate(peers):
            pltpu.make_async_remote_copy(
                src_ref=src.at[p, rows],
                dst_ref=dst.at[me, rows],
                send_sem=ssem.at[idx],
                recv_sem=rsem.at[idx],
                device_id=(seq, p),
                device_id_type=MESH,
            ).start()
            if i < len(between):
                between[i]()

    def send_by_row(src, dst, ssem, rsem, part, idx, passes):
        lo, hi = part
        rows = pl.ds(lo, hi - lo)
        for first, last in passes:
            for p in peers:

                @pl.when((p >= 4 * first) & (p < 4 * last))
                def _(p=p):
                    pltpu.make_async_remote_copy(
                        src_ref=src.at[p, rows],
                        dst_ref=dst.at[me, rows],
                        send_sem=ssem.at[idx],
                        recv_sem=rsem.at[idx],
                        device_id=(seq, p),
                        device_id_type=MESH,
                    ).start()

    def wait_all(buf, sem, part, idx):
        lo, hi = part
        view = buf.at[pl.ds(0, NB - 1), pl.ds(lo, hi - lo)]
        pltpu.make_async_copy(view, view, sem.at[idx]).wait()

    def head_cols(ref, h):
        return ref.at[:, pl.ds(pl.multiple_of(h * HD, HD), HD)]

    own = pltpu.make_async_copy(head_cols(v_hbm, me), v_raw.at[me], own_sem)
    own.start()
    pl.semaphore_wait(barrier, NB - 1 + 4)
    for p in peers:
        pltpu.make_async_remote_copy(
            src_ref=head_cols(v_hbm, p),
            dst_ref=v_raw.at[me],
            send_sem=v_ss,
            recv_sem=v_rs,
            device_id=(seq, p),
            device_id_type=MESH,
        ).start()
    rows = iota((BLK, BLK), 0)
    perm_ref[...] = (iota((BLK, BLK), 1) == ((rows & 15) << 4) + (rows >> 4)).astype(
        jnp.bfloat16
    )

    loads[0].wait()
    sort_rows(0, k_send)
    send(k_send, k_recv, k_ss, k_rs, K_PARTS[0], 0)
    loads[1].wait()
    sort_rows(1, q_send)
    send(q_send, q_recv, q_ss, q_rs, Q_PARTS[0], 0)
    send(k_send, k_recv, k_ss, k_rs, K_PARTS[1], 1)
    k_recv[me] = k_send[me]
    q_recv[me] = q_send[me]

    row_tok = token_of(iota((BLK, BLK), 0), me)
    col_tok = token_of(iota((BLK, BLK), 1), me)
    own_perm[...] = (iota((BLK, BLK), 1) == row_tok).astype(jnp.bfloat16)
    bias_ref[...] = jnp.where(col_tok <= row_tok, 0.0, LOW)
    for ref, period, level in ((mult0, 128, 0), (mult1, 128, 1), (mult2, 64, 2), (mult3, 32, 3)):
        shape = ref.shape
        both = jnp.minimum(
            class_of(iota(shape, 0)), class_of(iota(shape, 1) & (period - 1))
        )
        ref[...] = (1 + both - level).astype(jnp.float32)

    m_ref[0] = jnp.full(m_ref.shape[1:], LOW, jnp.float32)
    l_ref[0] = jnp.zeros(l_ref.shape[1:], jnp.float32)
    acc_ref[0] = jnp.zeros(acc_ref.shape[1:], jnp.float32)

    own.wait()
    arrived = v_raw.at[pl.ds(0, NB - 1)]
    pltpu.make_async_copy(arrived, arrived, v_rs).wait()
    for b in range(0, NB, 2):
        pair = jnp.dot(
            own_perm[...],
            jnp.concatenate([v_raw[b], v_raw[b + 1]], axis=1),
            preferred_element_type=jnp.float32,
        ).astype(jnp.bfloat16)
        v_recv[b] = pair[:, :HD]
        v_recv[b + 1] = pair[:, HD:]
    wait_all(k_recv, k_rs, K_PARTS[0], 0)

    def hop(src, dst, idx, target):
        return pltpu.make_async_remote_copy(
            src_ref=src,
            dst_ref=dst,
            send_sem=x_ss.at[idx],
            recv_sem=x_rs.at[idx],
            device_id=(target, me),
            device_id_type=MESH,
        )

    @pl.when(seq % 2 == 0)
    def _():
        hop(k_recv.at[:, pl.ds(0, 64)], kx2, 0, (seq // 2) * 2 + 1).start()
        hop(v_recv.at[:, pl.ds(0, 64)], vx2, 1, (seq // 2) * 2 + 1).start()

    near_chip = seq % 4 < 2
    far_chip = seq < 4

    def hop3(src, dst, idx):
        @pl.when(near_chip)
        def _():
            hop(src.at[:, pl.ds(0, 32)], dst.at[core], idx, (seq + 2) % 8).start()

    def hop4(src, dst, idx, step):
        @pl.when(far_chip)
        def _():
            target = 4 + 2 * step + core
            hop(src.at[:, pl.ds(0, 16)], dst.at[core, seq // 2 % 2], idx, target).start()

    hops = [functools.partial(hop3, *x) for x in ((k_recv, kx3, 2), (v_recv, vx3, 3))]
    hops += [
        functools.partial(hop4, *x, step)
        for step in range(2)
        for x in ((k_recv, kx4, 4), (v_recv, vx4, 5))
    ]
    send(q_send, q_recv, q_ss, q_rs, Q_PARTS[1], 1, between=hops)
    for i in range(2, NCH):
        send(q_send, q_recv, q_ss, q_rs, Q_PARTS[i], i)

    def hand_over():
        for here, pairs in (
            (jnp.logical_not(near_chip), ((kx3, 2), (vx3, 3))),
            (jnp.logical_not(far_chip), ((kx4, 4), (vx4, 5))),
        ):

            @pl.when(here)
            def _(pairs=pairs):
                for buf, idx in pairs:
                    hop(buf.at[core], buf.at[core], idx, partner).wait_recv()
                    hop(buf.at[core], buf.at[core], idx + 4, partner).start()

    def flash(chunk, blk0, nblk, rows, keys, vals, mask=False, mults=(), first=False):
        lo, hi = rows
        height = hi - lo
        length = nblk * height
        blocks = pl.ds(blk0, nblk)
        q = q_recv[blocks, pl.ds(chunk * CH + lo, height)].reshape(length, HD)
        s = lax.dot_general(
            q, keys, (((1,), (1,)), ((), ())), preferred_element_type=jnp.float32
        )
        if mask:
            s0 = s[:height] + bias_ref[pl.ds(chunk * CH + lo, height)]
            s = s0 if nblk == 1 else jnp.concatenate([s0, s[height:]], axis=0)
        width = keys.shape[0]
        lanes = [s[:, i : i + HD] for i in range(0, width, HD)]
        top = functools.reduce(jnp.maximum, lanes)
        top = jnp.broadcast_to(jnp.max(top, axis=1, keepdims=True), (length, HD))
        here = pl.ds(lo, height)
        state = min(chunk, 1)
        if not first:
            old = m_ref[state, blocks, here].reshape(length, HD)
            top = jnp.maximum(old, top)
            keep = jnp.exp2((old - top) * SCALE)
        m_ref[state, blocks, here] = top.reshape(nblk, height, HD)
        weights = []
        total = jnp.zeros((length, HD), jnp.float32)
        for i, part in enumerate(lanes):
            w = jnp.exp2((part - top) * SCALE)
            if i < len(mults) and mults[i] is not None:
                w = (w.reshape(nblk, height, HD) * mults[i][None]).reshape(length, HD)
            total = total + w
            weights.append(w.astype(jnp.bfloat16))
        pv = jnp.dot(
            jnp.concatenate(weights, axis=1), vals, preferred_element_type=jnp.float32
        )
        if not first:
            pv = pv + acc_ref[state, blocks, here].reshape(length, HD) * keep
            total = total + l_ref[state, blocks, here].reshape(length, HD) * keep
        acc_ref[state, blocks, here] = pv.reshape(nblk, height, HD)
        l_ref[state, blocks, here] = total.reshape(nblk, height, HD)

    def cross(chunk, blk0, nblk, rows, key_at, val_at, mult):
        for j in range(2):
            flash(chunk, blk0, nblk, rows, key_at(j), val_at(j), mults=[mult] * 4)

    wait_all(q_recv, q_rs, Q_PARTS[0], 0)

    @pl.when(seq % 2 == 1)
    def _():
        hop(kx2, kx2, 0, seq).wait_recv()
        hop(vx2, vx2, 1, seq).wait_recv()
        for g in range(2):
            cross(
                0, g * 8, 8, (0, 64),
                lambda j: kx2[pl.ds(j * 8, 8)].reshape(512, HD),
                lambda j: vx2[pl.ds(j * 8, 8)].reshape(512, HD),
                mult2[...],
            )

    def far_rows():
        @pl.when(seq % 4 >= 2)
        def _():
            hop(kx3.at[1 - core], kx3.at[1 - core], 6, partner).wait_recv()
            hop(vx3.at[1 - core], vx3.at[1 - core], 7, partner).wait_recv()
            cross(
                0, 0, NB, (0, 32),
                lambda j: kx3[j].reshape(512, HD),
                lambda j: vx3[j].reshape(512, HD),
                mult3[...],
            )

        @pl.when(seq >= 4)
        def _():
            hop(kx4.at[1 - core], kx4.at[1 - core], 8, partner).wait_recv()
            hop(vx4.at[1 - core], vx4.at[1 - core], 9, partner).wait_recv()
            cross(
                0, 0, NB, (0, 16),
                lambda j: kx4[j].reshape(512, HD),
                lambda j: vx4[j].reshape(512, HD),
                None,
            )

    wait_all(k_recv, k_rs, K_PARTS[1], 1)

    def own_rows(chunk):
        lo = chunk * CH
        nested = lo < 128

        def segment(g, carry):
            for kb in range(8):
                flash(
                    chunk, g * 8 + kb, 8 - kb, (0, CH),
                    k_recv[g * 8 + kb], v_recv[g * 8 + kb],
                    mask=True,
                    mults=[mult0[pl.ds(lo, CH)]] if nested else (),
                    first=chunk > 0 and kb == 0,
                )
            return carry

        segment(0, 0)
        segment(1, 0)
        if nested:
            cross(
                chunk, 8, 8, (0, CH),
                lambda j: k_recv[pl.ds(j * 4, 4), pl.ds(0, 128)].reshape(512, HD),
                lambda j: v_recv[pl.ds(j * 4, 4), pl.ds(0, 128)].reshape(512, HD),
                mult1[...] if chunk == 0 else None,
            )

    def finish(chunk):
        lo = chunk * CH
        state = min(chunk, 1)
        for b in range(NB):
            total = jnp.sum(l_ref[state, b], axis=1, keepdims=True)
            o_send[b, pl.ds(lo, CH)] = (acc_ref[state, b] / total).astype(jnp.bfloat16)
        o_recv[me, pl.ds(lo, CH)] = o_send[me, pl.ds(lo, CH)]
        if True:
            send_by_row(o_send, o_recv, o_ss, o_rs, Q_PARTS[chunk], chunk, [(0, 2), (2, 4)])
        else:
            send(o_send, o_recv, o_ss, o_rs, Q_PARTS[chunk], chunk)

    own_rows(0)
    for chunk in range(1, NCH):
        wait_all(q_recv, q_rs, Q_PARTS[chunk], chunk)
        own_rows(chunk)
        finish(chunk)
        if chunk == 1:
            hand_over()
        if chunk == FAR_AFTER:
            far_rows()
            finish(0)

    for i in range(NCH):
        wait_all(o_recv, o_rs, Q_PARTS[i], i)

    pltpu.make_async_copy(arrived, arrived, v_ss).wait()
    for i, part in enumerate(K_PARTS):
        wait_all(k_send, k_ss, part, i)
    for i, part in enumerate(Q_PARTS):
        wait_all(q_send, q_ss, part, i)
        wait_all(o_send, o_ss, part, i)

    for first, here, bufs in (
        (2, near_chip, (kx3.at[0], vx3.at[0])),
        (6, jnp.logical_not(near_chip), (kx3.at[0], vx3.at[0])),
        (4, far_chip, (kx4.at[0], vx4.at[0])),
        (8, jnp.logical_not(far_chip), (kx4.at[0], vx4.at[0])),
    ):

        @pl.when(here)
        def _(first=first, bufs=bufs):
            for i, buf in enumerate(bufs):
                hop(buf, buf, first + i, partner).wait_send()

    @pl.when(seq % 2 == 0)
    def _():
        hop(kx2, kx2, 0, seq).wait_send()
        hop(vx2, vx2, 1, seq).wait_send()


def unsort_kernel(o_ref, out_hbm, stage, sems):
    rows = iota((BLK, BLK), 0)
    perm = (iota((BLK, BLK), 1) == ((rows & 15) << 4) + (rows >> 4)).astype(jnp.bfloat16)
    copies = []
    for j in range(0, NB, 2):
        cols = []
        for h in (j, j + 1):
            groups = [SHIFTS.index((r - h) % 16) for r in range(16)]
            cols.append(
                jnp.concatenate([o_ref[h, g * 16 : (g + 1) * 16] for g in groups], axis=0)
            )
        stage[:, j * HD : (j + 2) * HD] = jnp.dot(
            perm, jnp.concatenate(cols, axis=1), preferred_element_type=jnp.float32
        ).astype(jnp.bfloat16)
        if j % 4 == 2:
            here = (slice(None), pl.ds((j - 2) * HD, 4 * HD))
            copy = pltpu.make_async_copy(stage.at[here], out_hbm.at[here], sems.at[j // 4])
            copy.start()
            copies.append(copy)
    for copy in copies:
        copy.wait()


def shards(queries, keys, values):
    bf, f32 = jnp.bfloat16, jnp.float32
    vm = pltpu.VMEM
    blocks = vm((NB, BLK, HD), bf)
    dma = pltpu.SemaphoreType.DMA
    nk = len(K_PARTS)
    queries, keys, values = (
        pltpu.with_memory_space_constraint(x, pltpu.HBM) for x in (queries, keys, values)
    )
    sorted_out = pl.pallas_call(
        kernel,
        out_shape=pltpu.VMEM((NB, BLK, HD), bf),
        in_specs=[pl.BlockSpec(memory_space=pltpu.HBM)] * 3,
        out_specs=pl.BlockSpec(memory_space=pltpu.VMEM),
        scratch_shapes=[
            vm((2, BLK, NB * HD), bf),
            *[blocks] * 7,
            vm((NB, 64, HD), bf), vm((NB, 64, HD), bf),
            vm((2, NB, 32, HD), bf), vm((2, NB, 32, HD), bf),
            vm((2, 2, NB, 16, HD), bf), vm((2, 2, NB, 16, HD), bf),
            *[vm((2, NB, CH, HD), f32)] * 3,
            vm((BLK, BLK), bf), vm((BLK, BLK), bf), vm((BLK, BLK), f32),
            vm((128, 128), f32), vm((64, 128), f32), vm((64, 128), f32), vm((32, 128), f32),
            dma((2,)), dma, dma((NCH,)), dma((nk,)), dma, dma((NCH,)),
            dma((NCH,)), dma((nk,)), dma, dma((NCH,)), dma((10,)), dma((10,)),
        ],
        compiler_params=pltpu.CompilerParams(
            collective_id=0, has_side_effects=True, vmem_limit_bytes=48 * 2**20
        ),
    )(queries, keys, values)
    sorted_out = pltpu.with_memory_space_constraint(sorted_out, pltpu.VMEM)
    return pl.pallas_call(
        unsort_kernel,
        out_shape=jax.ShapeDtypeStruct((BLK, NB * HD), bf),
        in_specs=[pl.BlockSpec(memory_space=pltpu.VMEM)],
        out_specs=pl.BlockSpec(memory_space=pl.ANY),
        scratch_shapes=[vm((BLK, NB * HD), bf), dma((4,))],
        compiler_params=pltpu.CompilerParams(vmem_limit_bytes=16 * 2**20),
    )(sorted_out)


def solution(mesh):
    spec = P(("seq", "head"), None)
    return jax.shard_map(
        shards, mesh=mesh, in_specs=(spec, spec, spec), out_specs=spec, check_vma=False
    )
```

```python
import functools
import math

import jax
import jax.numpy as jnp
from jax import lax
from jax.experimental import pallas as pl
from jax.experimental.pallas import tpu as pltpu
from jax.sharding import PartitionSpec as P

HD = 128
BLK = 256
NB = 16
CH = 64
NCH = BLK // CH
SPLIT = (1, 2, 3)
FAR_AFTER = 2
SCALE = HD**-0.5 * math.log2(math.e)
LOW = -1e30
MESH = pl.DeviceIdType.MESH

ORDER = [
    (1, 2), (3, 2), (2, 1), (2, 3),
    (0, 1), (0, 3), (1, 0), (3, 0),
    (2, 2), (1, 1), (3, 3),
    (0, 2), (2, 0), (1, 3), (3, 1),
]

K_PARTS = [(0, 64), (64, 256)]
Q_PARTS = [(i * CH, (i + 1) * CH) for i in range(NCH)]


SHIFTS = [0, 8, 4, 12, 2, 6, 10, 14, 1, 3, 5, 7, 9, 11, 13, 15]


def token_of(row, head):
    group = row >> 4
    shift = jnp.where(
        group >= 8,
        1 + ((group - 8) << 1),
        jnp.where(
            group >= 4,
            2 + ((group - 4) << 2),
            jnp.where(group >= 2, 4 + ((group - 2) << 3), jnp.where(group >= 1, 8, 0)),
        ),
    )
    return ((row & 15) << 4) + ((shift + head) & 15)


def class_of(row):
    return (
        (row < 128).astype(jnp.int32)
        + (row < 64).astype(jnp.int32)
        + (row < 32).astype(jnp.int32)
        + (row < 16).astype(jnp.int32)
    )


def iota(shape, dim):
    return lax.broadcasted_iota(jnp.int32, shape, dim)


def kernel(
    q_hbm, k_hbm, v_hbm, o_recv,
    x_in, q_send, k_send, v_raw, q_recv, k_recv, v_recv, o_send,
    kx2, vx2, kx3, vx3, kx4, vx4,
    m_ref, l_ref, acc_ref, perm_ref, own_perm, bias_ref, mult0, mult1, mult2, mult3,
    in_sem, own_sem, q_ss, k_ss, v_ss, o_ss, q_rs, k_rs, v_rs, o_rs, x_ss, x_rs,
):
    seq = lax.axis_index("seq")
    me = lax.axis_index("head")
    z, y = me // 4, me % 4
    flip = 1 + 2 * (seq % 2)
    peers = [((z + dz * flip) % 4) * 4 + (y + dy * flip) % 4 for dz, dy in ORDER]

    barrier = pltpu.get_barrier_semaphore()
    for p in peers:
        pl.semaphore_signal(barrier, inc=1, device_id=(seq, p), device_id_type=MESH)
    core = seq % 2
    partner = seq + 1 - 2 * core
    other_half = (seq // 4 + 1) % 2 * 4 + core
    beside = seq + 2 - 4 * (seq // 2 % 2)
    for t in (partner, beside, other_half, other_half + 2):
        pl.semaphore_signal(barrier, inc=1, device_id=(t, me), device_id_type=MESH)

    loads = []
    for i, src in enumerate((k_hbm, q_hbm)):
        cp = pltpu.make_async_copy(src, x_in.at[i], in_sem.at[i])
        cp.start()
        loads.append(cp)

    def sort_rows(i, dst):
        for j in range(0, NB, 2):
            pair = jnp.dot(
                perm_ref[...],
                x_in[i, :, j * HD : (j + 2) * HD],
                preferred_element_type=jnp.float32,
            ).astype(jnp.bfloat16)
            for h in (j, j + 1):
                cols = pair[:, (h - j) * HD : (h - j + 1) * HD]
                for g, shift in enumerate(SHIFTS):
                    r = (h + shift) % 16
                    dst[h, g * 16 : (g + 1) * 16] = cols[r * 16 : (r + 1) * 16]

    def send(src, dst, ssem, rsem, part, idx, between=()):
        lo, hi = part
        rows = pl.ds(lo, hi - lo)
        for i, p in enumerate(peers):
            pltpu.make_async_remote_copy(
                src_ref=src.at[p, rows],
                dst_ref=dst.at[me, rows],
                send_sem=ssem.at[idx],
                recv_sem=rsem.at[idx],
                device_id=(seq, p),
                device_id_type=MESH,
            ).start()
            if i < len(between):
                between[i]()

    def send_by_row(src, dst, ssem, rsem, part, idx, passes):
        lo, hi = part
        rows = pl.ds(lo, hi - lo)
        for first, last in passes:
            for p in peers:

                @pl.when((p >= 4 * first) & (p < 4 * last))
                def _(p=p):
                    pltpu.make_async_remote_copy(
                        src_ref=src.at[p, rows],
                        dst_ref=dst.at[me, rows],
                        send_sem=ssem.at[idx],
                        recv_sem=rsem.at[idx],
                        device_id=(seq, p),
                        device_id_type=MESH,
                    ).start()

    def wait_all(buf, sem, part, idx):
        lo, hi = part
        view = buf.at[pl.ds(0, NB - 1), pl.ds(lo, hi - lo)]
        pltpu.make_async_copy(view, view, sem.at[idx]).wait()

    def head_cols(ref, h):
        return ref.at[:, pl.ds(pl.multiple_of(h * HD, HD), HD)]

    own = pltpu.make_async_copy(head_cols(v_hbm, me), v_raw.at[me], own_sem)
    own.start()
    pl.semaphore_wait(barrier, NB - 1 + 4)
    for p in peers:
        pltpu.make_async_remote_copy(
            src_ref=head_cols(v_hbm, p),
            dst_ref=v_raw.at[me],
            send_sem=v_ss,
            recv_sem=v_rs,
            device_id=(seq, p),
            device_id_type=MESH,
        ).start()
    rows = iota((BLK, BLK), 0)
    perm_ref[...] = (iota((BLK, BLK), 1) == ((rows & 15) << 4) + (rows >> 4)).astype(
        jnp.bfloat16
    )

    loads[0].wait()
    sort_rows(0, k_send)
    send(k_send, k_recv, k_ss, k_rs, K_PARTS[0], 0)
    loads[1].wait()
    sort_rows(1, q_send)
    send(q_send, q_recv, q_ss, q_rs, Q_PARTS[0], 0)
    send(k_send, k_recv, k_ss, k_rs, K_PARTS[1], 1)
    k_recv[me] = k_send[me]
    q_recv[me] = q_send[me]

    row_tok = token_of(iota((BLK, BLK), 0), me)
    col_tok = token_of(iota((BLK, BLK), 1), me)
    own_perm[...] = (iota((BLK, BLK), 1) == row_tok).astype(jnp.bfloat16)
    bias_ref[...] = jnp.where(col_tok <= row_tok, 0.0, LOW)
    for ref, period, level in ((mult0, 128, 0), (mult1, 128, 1), (mult2, 64, 2), (mult3, 32, 3)):
        shape = ref.shape
        both = jnp.minimum(
            class_of(iota(shape, 0)), class_of(iota(shape, 1) & (period - 1))
        )
        ref[...] = (1 + both - level).astype(jnp.float32)

    m_ref[0] = jnp.full(m_ref.shape[1:], LOW, jnp.float32)
    l_ref[0] = jnp.zeros(l_ref.shape[1:], jnp.float32)
    acc_ref[0] = jnp.zeros(acc_ref.shape[1:], jnp.float32)

    own.wait()
    arrived = v_raw.at[pl.ds(0, NB - 1)]
    pltpu.make_async_copy(arrived, arrived, v_rs).wait()
    for b in range(0, NB, 2):
        pair = jnp.dot(
            own_perm[...],
            jnp.concatenate([v_raw[b], v_raw[b + 1]], axis=1),
            preferred_element_type=jnp.float32,
        ).astype(jnp.bfloat16)
        v_recv[b] = pair[:, :HD]
        v_recv[b + 1] = pair[:, HD:]
    wait_all(k_recv, k_rs, K_PARTS[0], 0)

    def hop(src, dst, idx, target):
        return pltpu.make_async_remote_copy(
            src_ref=src,
            dst_ref=dst,
            send_sem=x_ss.at[idx],
            recv_sem=x_rs.at[idx],
            device_id=(target, me),
            device_id_type=MESH,
        )

    near_chip = seq % 4 < 2
    far_chip = seq < 4

    def hop3(src, dst, idx):
        @pl.when(near_chip)
        def _():
            hop(src.at[:, pl.ds(0, 32)], dst.at[core], idx, (seq + 2) % 8).start()

    def hop4(src, dst, idx, step):
        @pl.when(far_chip)
        def _():
            target = 4 + 2 * step + core
            hop(src.at[:, pl.ds(0, 16)], dst.at[core, seq // 2 % 2], idx, target).start()

    def hop2(src, dst, idx):
        @pl.when(core == 0)
        def _():
            hop(src.at[:, pl.ds(0, 64)], dst, idx, partner).start()

    hops = [functools.partial(hop3, *x) for x in ((k_recv, kx3, 2), (v_recv, vx3, 3))]
    hops += [
        functools.partial(hop4, *x, step)
        for step in range(2)
        for x in ((k_recv, kx4, 4), (v_recv, vx4, 5))
    ]
    hops += [functools.partial(hop2, *x) for x in ((k_recv, kx2, 0), (v_recv, vx2, 1))]
    send(q_send, q_recv, q_ss, q_rs, Q_PARTS[1], 1, between=hops)
    for i in range(2, NCH):
        send(q_send, q_recv, q_ss, q_rs, Q_PARTS[i], i)

    def hand_over():
        for here, pairs in (
            (jnp.logical_not(near_chip), ((kx3, 2), (vx3, 3))),
            (jnp.logical_not(far_chip), ((kx4, 4), (vx4, 5))),
        ):

            @pl.when(here)
            def _(pairs=pairs):
                for buf, idx in pairs:
                    hop(buf.at[core], buf.at[core], idx, partner).wait_recv()
                    hop(buf.at[core], buf.at[core], idx + 4, partner).start()

    def flash(chunk, blk0, nblk, rows, keys, vals, mask=False, mults=(), first=False):
        lo, hi = rows
        height = hi - lo
        length = nblk * height
        blocks = pl.ds(blk0, nblk)
        q = q_recv[blocks, pl.ds(chunk * CH + lo, height)].reshape(length, HD)
        s = lax.dot_general(
            q, keys, (((1,), (1,)), ((), ())), preferred_element_type=jnp.float32
        )
        if mask:
            s0 = s[:height] + bias_ref[pl.ds(chunk * CH + lo, height)]
            s = s0 if nblk == 1 else jnp.concatenate([s0, s[height:]], axis=0)
        width = keys.shape[0]
        lanes = [s[:, i : i + HD] for i in range(0, width, HD)]
        top = functools.reduce(jnp.maximum, lanes)
        top = jnp.broadcast_to(jnp.max(top, axis=1, keepdims=True), (length, HD))
        here = pl.ds(lo, height)
        state = min(chunk, 1)
        if not first:
            old = m_ref[state, blocks, here].reshape(length, HD)
            top = jnp.maximum(old, top)
            keep = jnp.exp2((old - top) * SCALE)
        m_ref[state, blocks, here] = top.reshape(nblk, height, HD)
        weights = []
        total = jnp.zeros((length, HD), jnp.float32)
        for i, part in enumerate(lanes):
            w = jnp.exp2((part - top) * SCALE)
            if i < len(mults) and mults[i] is not None:
                w = (w.reshape(nblk, height, HD) * mults[i][None]).reshape(length, HD)
            total = total + w
            weights.append(w.astype(jnp.bfloat16))
        pv = jnp.dot(
            jnp.concatenate(weights, axis=1), vals, preferred_element_type=jnp.float32
        )
        if not first:
            pv = pv + acc_ref[state, blocks, here].reshape(length, HD) * keep
            total = total + l_ref[state, blocks, here].reshape(length, HD) * keep
        acc_ref[state, blocks, here] = pv.reshape(nblk, height, HD)
        l_ref[state, blocks, here] = total.reshape(nblk, height, HD)

    def cross(chunk, blk0, nblk, rows, key_at, val_at, mult):
        for j in range(2):
            flash(chunk, blk0, nblk, rows, key_at(j), val_at(j), mults=[mult] * 4)

    wait_all(q_recv, q_rs, Q_PARTS[0], 0)

    @pl.when(seq % 2 == 1)
    def _():
        hop(kx2, kx2, 0, seq).wait_recv()
        hop(vx2, vx2, 1, seq).wait_recv()
        for g in range(2):
            cross(
                0, g * 8, 8, (0, 64),
                lambda j: kx2[pl.ds(j * 8, 8)].reshape(512, HD),
                lambda j: vx2[pl.ds(j * 8, 8)].reshape(512, HD),
                mult2[...],
            )

    def far_rows():
        @pl.when(seq % 4 >= 2)
        def _():
            hop(kx3.at[1 - core], kx3.at[1 - core], 6, partner).wait_recv()
            hop(vx3.at[1 - core], vx3.at[1 - core], 7, partner).wait_recv()
            cross(
                0, 0, NB, (0, 32),
                lambda j: kx3[j].reshape(512, HD),
                lambda j: vx3[j].reshape(512, HD),
                mult3[...],
            )

        @pl.when(seq >= 4)
        def _():
            hop(kx4.at[1 - core], kx4.at[1 - core], 8, partner).wait_recv()
            hop(vx4.at[1 - core], vx4.at[1 - core], 9, partner).wait_recv()
            cross(
                0, 0, NB, (0, 16),
                lambda j: kx4[j].reshape(512, HD),
                lambda j: vx4[j].reshape(512, HD),
                None,
            )

    wait_all(k_recv, k_rs, K_PARTS[1], 1)

    def own_rows(chunk, between=None):
        lo = chunk * CH
        nested = lo < 128

        def segment(g, carry):
            for kb in range(8):
                flash(
                    chunk, g * 8 + kb, 8 - kb, (0, CH),
                    k_recv[g * 8 + kb], v_recv[g * 8 + kb],
                    mask=True,
                    mults=[mult0[pl.ds(lo, CH)]] if nested else (),
                    first=chunk > 0 and kb == 0,
                )
            return carry

        segment(0, 0)
        if between is not None:
            between()
        segment(1, 0)
        if nested:
            cross(
                chunk, 8, 8, (0, CH),
                lambda j: k_recv[pl.ds(j * 4, 4), pl.ds(0, 128)].reshape(512, HD),
                lambda j: v_recv[pl.ds(j * 4, 4), pl.ds(0, 128)].reshape(512, HD),
                mult1[...] if chunk == 0 else None,
            )

    def finish(chunk, first=0, last=4):
        lo = chunk * CH
        state = min(chunk, 1)
        for b in range(4 * first, 4 * last):
            total = jnp.sum(l_ref[state, b], axis=1, keepdims=True)
            o_send[b, pl.ds(lo, CH)] = (acc_ref[state, b] / total).astype(jnp.bfloat16)

        @pl.when((me >= 4 * first) & (me < 4 * last))
        def _():
            o_recv[me, pl.ds(lo, CH)] = o_send[me, pl.ds(lo, CH)]

        passes = [(i, i + 2) for i in range(first, last, 2)]
        send_by_row(o_send, o_recv, o_ss, o_rs, Q_PARTS[chunk], chunk, passes)

    own_rows(0)
    for chunk in range(1, NCH):
        wait_all(q_recv, q_rs, Q_PARTS[chunk], chunk)
        if chunk in SPLIT:
            own_rows(chunk, functools.partial(finish, chunk, 0, 2))
            finish(chunk, 2, 4)
        else:
            own_rows(chunk)
            finish(chunk)
        if chunk == 1:
            hand_over()
        if chunk == FAR_AFTER:
            far_rows()
            finish(0)

    for i in range(NCH):
        wait_all(o_recv, o_rs, Q_PARTS[i], i)

    pltpu.make_async_copy(arrived, arrived, v_ss).wait()
    for i, part in enumerate(K_PARTS):
        wait_all(k_send, k_ss, part, i)
    for i, part in enumerate(Q_PARTS):
        wait_all(q_send, q_ss, part, i)
        wait_all(o_send, o_ss, part, i)

    for first, here, bufs in (
        (2, near_chip, (kx3.at[0], vx3.at[0])),
        (6, jnp.logical_not(near_chip), (kx3.at[0], vx3.at[0])),
        (4, far_chip, (kx4.at[0], vx4.at[0])),
        (8, jnp.logical_not(far_chip), (kx4.at[0], vx4.at[0])),
    ):

        @pl.when(here)
        def _(first=first, bufs=bufs):
            for i, buf in enumerate(bufs):
                hop(buf, buf, first + i, partner).wait_send()

    @pl.when(seq % 2 == 0)
    def _():
        hop(kx2, kx2, 0, seq).wait_send()
        hop(vx2, vx2, 1, seq).wait_send()


def unsort_kernel(o_ref, out_hbm, stage, sems):
    rows = iota((BLK, BLK), 0)
    perm = (iota((BLK, BLK), 1) == ((rows & 15) << 4) + (rows >> 4)).astype(jnp.bfloat16)
    copies = []
    for j in range(0, NB, 2):
        cols = []
        for h in (j, j + 1):
            groups = [SHIFTS.index((r - h) % 16) for r in range(16)]
            cols.append(
                jnp.concatenate([o_ref[h, g * 16 : (g + 1) * 16] for g in groups], axis=0)
            )
        stage[:, j * HD : (j + 2) * HD] = jnp.dot(
            perm, jnp.concatenate(cols, axis=1), preferred_element_type=jnp.float32
        ).astype(jnp.bfloat16)
        if j % 4 == 2:
            here = (slice(None), pl.ds((j - 2) * HD, 4 * HD))
            copy = pltpu.make_async_copy(stage.at[here], out_hbm.at[here], sems.at[j // 4])
            copy.start()
            copies.append(copy)
    for copy in copies:
        copy.wait()


def shards(queries, keys, values):
    bf, f32 = jnp.bfloat16, jnp.float32
    vm = pltpu.VMEM
    blocks = vm((NB, BLK, HD), bf)
    dma = pltpu.SemaphoreType.DMA
    nk = len(K_PARTS)
    queries, keys, values = (
        pltpu.with_memory_space_constraint(x, pltpu.HBM) for x in (queries, keys, values)
    )
    sorted_out = pl.pallas_call(
        kernel,
        out_shape=pltpu.VMEM((NB, BLK, HD), bf),
        in_specs=[pl.BlockSpec(memory_space=pltpu.HBM)] * 3,
        out_specs=pl.BlockSpec(memory_space=pltpu.VMEM),
        scratch_shapes=[
            vm((2, BLK, NB * HD), bf),
            *[blocks] * 7,
            vm((NB, 64, HD), bf), vm((NB, 64, HD), bf),
            vm((2, NB, 32, HD), bf), vm((2, NB, 32, HD), bf),
            vm((2, 2, NB, 16, HD), bf), vm((2, 2, NB, 16, HD), bf),
            *[vm((2, NB, CH, HD), f32)] * 3,
            vm((BLK, BLK), bf), vm((BLK, BLK), bf), vm((BLK, BLK), f32),
            vm((128, 128), f32), vm((64, 128), f32), vm((64, 128), f32), vm((32, 128), f32),
            dma((2,)), dma, dma((NCH,)), dma((nk,)), dma, dma((NCH,)),
            dma((NCH,)), dma((nk,)), dma, dma((NCH,)), dma((10,)), dma((10,)),
        ],
        compiler_params=pltpu.CompilerParams(
            collective_id=0, has_side_effects=True, vmem_limit_bytes=48 * 2**20
        ),
    )(queries, keys, values)
    sorted_out = pltpu.with_memory_space_constraint(sorted_out, pltpu.VMEM)
    return pl.pallas_call(
        unsort_kernel,
        out_shape=jax.ShapeDtypeStruct((BLK, NB * HD), bf),
        in_specs=[pl.BlockSpec(memory_space=pltpu.VMEM)],
        out_specs=pl.BlockSpec(memory_space=pl.ANY),
        scratch_shapes=[vm((BLK, NB * HD), bf), dma((4,))],
        compiler_params=pltpu.CompilerParams(vmem_limit_bytes=16 * 2**20),
    )(sorted_out)


def solution(mesh):
    spec = P(("seq", "head"), None)
    return jax.shard_map(
        shards, mesh=mesh, in_specs=(spec, spec, spec), out_specs=spec, check_vma=False
    )
```

```python
import functools
import math

import jax
import jax.numpy as jnp
from jax import lax
from jax.experimental import pallas as pl
from jax.experimental.pallas import tpu as pltpu
from jax.sharding import PartitionSpec as P

HD = 128
BLK = 256
NB = 16
CH = 64
NCH = BLK // CH
SPLIT = (1, 2, 3)
FAR_AFTER = 2
SCALE = HD**-0.5 * math.log2(math.e)
LOW = -1e30
MESH = pl.DeviceIdType.MESH

ORDER = [
    (1, 2), (3, 2), (2, 1), (2, 3),
    (0, 1), (0, 3), (1, 0), (3, 0),
    (2, 2), (1, 1), (3, 3),
    (0, 2), (2, 0), (1, 3), (3, 1),
]

K_PARTS = [(0, 64), (64, 256)]
Q_PARTS = [(i * CH, (i + 1) * CH) for i in range(NCH)]


SHIFTS = [0, 8, 4, 12, 2, 6, 10, 14, 1, 3, 5, 7, 9, 11, 13, 15]


def token_of(row, head):
    group = row >> 4
    shift = jnp.where(
        group >= 8,
        1 + ((group - 8) << 1),
        jnp.where(
            group >= 4,
            2 + ((group - 4) << 2),
            jnp.where(group >= 2, 4 + ((group - 2) << 3), jnp.where(group >= 1, 8, 0)),
        ),
    )
    return ((row & 15) << 4) + ((shift + head) & 15)


def class_of(row):
    return (
        (row < 128).astype(jnp.int32)
        + (row < 64).astype(jnp.int32)
        + (row < 32).astype(jnp.int32)
        + (row < 16).astype(jnp.int32)
    )


def iota(shape, dim):
    return lax.broadcasted_iota(jnp.int32, shape, dim)


def kernel(
    q_hbm, k_hbm, v_hbm, o_recv,
    x_in, q_send, k_send, v_raw, q_recv, k_recv, v_recv, o_send,
    kx2, vx2, kx3, vx3, kx4, vx4,
    m_ref, l_ref, acc_ref, perm_ref, own_perm, bias_ref, mult0, mult1, mult2, mult3,
    in_sem, own_sem, q_ss, k_ss, v_ss, o_ss, q_rs, k_rs, v_rs, o_rs, x_ss, x_rs,
):
    seq = lax.axis_index("seq")
    me = lax.axis_index("head")
    z, y = me // 4, me % 4
    flip = 1 + 2 * (seq % 2)
    peers = [((z + dz * flip) % 4) * 4 + (y + dy * flip) % 4 for dz, dy in ORDER]

    barrier = pltpu.get_barrier_semaphore()
    for p in peers:
        pl.semaphore_signal(barrier, inc=1, device_id=(seq, p), device_id_type=MESH)
    core = seq % 2
    partner = seq + 1 - 2 * core
    other_half = (seq // 4 + 1) % 2 * 4 + core
    beside = seq + 2 - 4 * (seq // 2 % 2)
    for t in (partner, beside, other_half, other_half + 2):
        pl.semaphore_signal(barrier, inc=1, device_id=(t, me), device_id_type=MESH)

    loads = []
    for i, src in enumerate((k_hbm, q_hbm)):
        cp = pltpu.make_async_copy(src, x_in.at[i], in_sem.at[i])
        loads.append(cp)
    loads[0].start()

    def sort_rows(i, dst):
        for j in range(0, NB, 2):
            pair = jnp.dot(
                perm_ref[...],
                x_in[i, :, j * HD : (j + 2) * HD],
                preferred_element_type=jnp.float32,
            ).astype(jnp.bfloat16)
            for h in (j, j + 1):
                cols = pair[:, (h - j) * HD : (h - j + 1) * HD]
                for g, shift in enumerate(SHIFTS):
                    r = (h + shift) % 16
                    dst[h, g * 16 : (g + 1) * 16] = cols[r * 16 : (r + 1) * 16]

    def send(src, dst, ssem, rsem, part, idx, between=()):
        lo, hi = part
        rows = pl.ds(lo, hi - lo)
        for i, p in enumerate(peers):
            pltpu.make_async_remote_copy(
                src_ref=src.at[p, rows],
                dst_ref=dst.at[me, rows],
                send_sem=ssem.at[idx],
                recv_sem=rsem.at[idx],
                device_id=(seq, p),
                device_id_type=MESH,
            ).start()
            if i < len(between):
                between[i]()

    def send_by_row(src, dst, ssem, rsem, part, idx, passes):
        lo, hi = part
        rows = pl.ds(lo, hi - lo)
        for first, last in passes:
            for p in peers:

                @pl.when((p >= 4 * first) & (p < 4 * last))
                def _(p=p):
                    pltpu.make_async_remote_copy(
                        src_ref=src.at[p, rows],
                        dst_ref=dst.at[me, rows],
                        send_sem=ssem.at[idx],
                        recv_sem=rsem.at[idx],
                        device_id=(seq, p),
                        device_id_type=MESH,
                    ).start()

    def wait_all(buf, sem, part, idx):
        lo, hi = part
        view = buf.at[pl.ds(0, NB - 1), pl.ds(lo, hi - lo)]
        pltpu.make_async_copy(view, view, sem.at[idx]).wait()

    def head_cols(ref, h):
        return ref.at[:, pl.ds(pl.multiple_of(h * HD, HD), HD)]

    own = pltpu.make_async_copy(head_cols(v_hbm, me), v_raw.at[me], own_sem)
    own.start()
    pl.semaphore_wait(barrier, NB - 1 + 4)
    for p in peers:
        pltpu.make_async_remote_copy(
            src_ref=head_cols(v_hbm, p),
            dst_ref=v_raw.at[me],
            send_sem=v_ss,
            recv_sem=v_rs,
            device_id=(seq, p),
            device_id_type=MESH,
        ).start()
    loads[1].start()

    rows = iota((BLK, BLK), 0)
    perm_ref[...] = (iota((BLK, BLK), 1) == ((rows & 15) << 4) + (rows >> 4)).astype(
        jnp.bfloat16
    )

    loads[0].wait()
    sort_rows(0, k_send)
    send(k_send, k_recv, k_ss, k_rs, K_PARTS[0], 0)
    loads[1].wait()
    sort_rows(1, q_send)
    send(q_send, q_recv, q_ss, q_rs, Q_PARTS[0], 0)
    send(k_send, k_recv, k_ss, k_rs, K_PARTS[1], 1)
    k_recv[me] = k_send[me]
    q_recv[me] = q_send[me]

    row_tok = token_of(iota((BLK, BLK), 0), me)
    col_tok = token_of(iota((BLK, BLK), 1), me)
    own_perm[...] = (iota((BLK, BLK), 1) == row_tok).astype(jnp.bfloat16)
    bias_ref[...] = jnp.where(col_tok <= row_tok, 0.0, LOW)
    for ref, period, level in ((mult0, 128, 0), (mult1, 128, 1), (mult2, 64, 2), (mult3, 32, 3)):
        shape = ref.shape
        both = jnp.minimum(
            class_of(iota(shape, 0)), class_of(iota(shape, 1) & (period - 1))
        )
        ref[...] = (1 + both - level).astype(jnp.float32)

    m_ref[0] = jnp.full(m_ref.shape[1:], LOW, jnp.float32)
    l_ref[0] = jnp.zeros(l_ref.shape[1:], jnp.float32)
    acc_ref[0] = jnp.zeros(acc_ref.shape[1:], jnp.float32)

    own.wait()
    arrived = v_raw.at[pl.ds(0, NB - 1)]
    pltpu.make_async_copy(arrived, arrived, v_rs).wait()
    for b in range(0, NB, 2):
        pair = jnp.dot(
            own_perm[...],
            jnp.concatenate([v_raw[b], v_raw[b + 1]], axis=1),
            preferred_element_type=jnp.float32,
        ).astype(jnp.bfloat16)
        v_recv[b] = pair[:, :HD]
        v_recv[b + 1] = pair[:, HD:]
    wait_all(k_recv, k_rs, K_PARTS[0], 0)

    def hop(src, dst, idx, target):
        return pltpu.make_async_remote_copy(
            src_ref=src,
            dst_ref=dst,
            send_sem=x_ss.at[idx],
            recv_sem=x_rs.at[idx],
            device_id=(target, me),
            device_id_type=MESH,
        )

    near_chip = seq % 4 < 2
    far_chip = seq < 4

    def hop3(src, dst, idx):
        @pl.when(near_chip)
        def _():
            hop(src.at[:, pl.ds(0, 32)], dst.at[core], idx, (seq + 2) % 8).start()

    def hop4(src, dst, idx, step):
        @pl.when(far_chip)
        def _():
            target = 4 + 2 * step + core
            hop(src.at[:, pl.ds(0, 16)], dst.at[core, seq // 2 % 2], idx, target).start()

    def hop2(src, dst, idx):
        @pl.when(core == 0)
        def _():
            hop(src.at[:, pl.ds(0, 64)], dst, idx, partner).start()

    hops = [functools.partial(hop3, *x) for x in ((k_recv, kx3, 2), (v_recv, vx3, 3))]
    hops += [
        functools.partial(hop4, *x, step)
        for step in range(2)
        for x in ((k_recv, kx4, 4), (v_recv, vx4, 5))
    ]
    hops += [functools.partial(hop2, *x) for x in ((k_recv, kx2, 0), (v_recv, vx2, 1))]
    send(q_send, q_recv, q_ss, q_rs, Q_PARTS[1], 1, between=hops)
    for i in range(2, NCH):
        send(q_send, q_recv, q_ss, q_rs, Q_PARTS[i], i)

    def hand_over():
        for here, pairs in (
            (jnp.logical_not(near_chip), ((kx3, 2), (vx3, 3))),
            (jnp.logical_not(far_chip), ((kx4, 4), (vx4, 5))),
        ):

            @pl.when(here)
            def _(pairs=pairs):
                for buf, idx in pairs:
                    hop(buf.at[core], buf.at[core], idx, partner).wait_recv()
                    hop(buf.at[core], buf.at[core], idx + 4, partner).start()

    def flash(chunk, blk0, nblk, rows, keys, vals, mask=False, mults=(), first=False):
        lo, hi = rows
        height = hi - lo
        length = nblk * height
        blocks = pl.ds(blk0, nblk)
        q = q_recv[blocks, pl.ds(chunk * CH + lo, height)].reshape(length, HD)
        s = lax.dot_general(
            q, keys, (((1,), (1,)), ((), ())), preferred_element_type=jnp.float32
        )
        if mask:
            s0 = s[:height] + bias_ref[pl.ds(chunk * CH + lo, height)]
            s = s0 if nblk == 1 else jnp.concatenate([s0, s[height:]], axis=0)
        width = keys.shape[0]
        lanes = [s[:, i : i + HD] for i in range(0, width, HD)]
        top = functools.reduce(jnp.maximum, lanes)
        top = jnp.broadcast_to(jnp.max(top, axis=1, keepdims=True), (length, HD))
        here = pl.ds(lo, height)
        state = min(chunk, 1)
        if not first:
            old = m_ref[state, blocks, here].reshape(length, HD)
            top = jnp.maximum(old, top)
            keep = jnp.exp2((old - top) * SCALE)
        m_ref[state, blocks, here] = top.reshape(nblk, height, HD)
        weights = []
        total = jnp.zeros((length, HD), jnp.float32)
        for i, part in enumerate(lanes):
            w = jnp.exp2((part - top) * SCALE)
            if i < len(mults) and mults[i] is not None:
                w = (w.reshape(nblk, height, HD) * mults[i][None]).reshape(length, HD)
            total = total + w
            weights.append(w.astype(jnp.bfloat16))
        pv = jnp.dot(
            jnp.concatenate(weights, axis=1), vals, preferred_element_type=jnp.float32
        )
        if not first:
            pv = pv + acc_ref[state, blocks, here].reshape(length, HD) * keep
            total = total + l_ref[state, blocks, here].reshape(length, HD) * keep
        acc_ref[state, blocks, here] = pv.reshape(nblk, height, HD)
        l_ref[state, blocks, here] = total.reshape(nblk, height, HD)

    def cross(chunk, blk0, nblk, rows, key_at, val_at, mult):
        for j in range(2):
            flash(chunk, blk0, nblk, rows, key_at(j), val_at(j), mults=[mult] * 4)

    wait_all(q_recv, q_rs, Q_PARTS[0], 0)

    @pl.when(seq % 2 == 1)
    def _():
        hop(kx2, kx2, 0, seq).wait_recv()
        hop(vx2, vx2, 1, seq).wait_recv()
        for g in range(2):
            cross(
                0, g * 8, 8, (0, 64),
                lambda j: kx2[pl.ds(j * 8, 8)].reshape(512, HD),
                lambda j: vx2[pl.ds(j * 8, 8)].reshape(512, HD),
                mult2[...],
            )

    def far_rows():
        @pl.when(seq % 4 >= 2)
        def _():
            hop(kx3.at[1 - core], kx3.at[1 - core], 6, partner).wait_recv()
            hop(vx3.at[1 - core], vx3.at[1 - core], 7, partner).wait_recv()
            cross(
                0, 0, NB, (0, 32),
                lambda j: kx3[j].reshape(512, HD),
                lambda j: vx3[j].reshape(512, HD),
                mult3[...],
            )

        @pl.when(seq >= 4)
        def _():
            hop(kx4.at[1 - core], kx4.at[1 - core], 8, partner).wait_recv()
            hop(vx4.at[1 - core], vx4.at[1 - core], 9, partner).wait_recv()
            cross(
                0, 0, NB, (0, 16),
                lambda j: kx4[j].reshape(512, HD),
                lambda j: vx4[j].reshape(512, HD),
                None,
            )

    wait_all(k_recv, k_rs, K_PARTS[1], 1)

    def own_rows(chunk, between=None):
        lo = chunk * CH
        nested = lo < 128

        def segment(g, carry):
            for kb in range(8):
                flash(
                    chunk, g * 8 + kb, 8 - kb, (0, CH),
                    k_recv[g * 8 + kb], v_recv[g * 8 + kb],
                    mask=True,
                    mults=[mult0[pl.ds(lo, CH)]] if nested else (),
                    first=chunk > 0 and kb == 0,
                )
            return carry

        segment(0, 0)
        if between is not None:
            between()
        segment(1, 0)
        if nested:
            cross(
                chunk, 8, 8, (0, CH),
                lambda j: k_recv[pl.ds(j * 4, 4), pl.ds(0, 128)].reshape(512, HD),
                lambda j: v_recv[pl.ds(j * 4, 4), pl.ds(0, 128)].reshape(512, HD),
                mult1[...] if chunk == 0 else None,
            )

    def finish(chunk, first=0, last=4):
        lo = chunk * CH
        state = min(chunk, 1)
        for b in range(4 * first, 4 * last):
            total = jnp.sum(l_ref[state, b], axis=1, keepdims=True)
            o_send[b, pl.ds(lo, CH)] = (acc_ref[state, b] / total).astype(jnp.bfloat16)

        @pl.when((me >= 4 * first) & (me < 4 * last))
        def _():
            o_recv[me, pl.ds(lo, CH)] = o_send[me, pl.ds(lo, CH)]

        passes = [(i, i + 2) for i in range(first, last, 2)]
        send_by_row(o_send, o_recv, o_ss, o_rs, Q_PARTS[chunk], chunk, passes)

    own_rows(0)
    for chunk in range(1, NCH):
        wait_all(q_recv, q_rs, Q_PARTS[chunk], chunk)
        if chunk in SPLIT:
            own_rows(chunk, functools.partial(finish, chunk, 0, 2))
            finish(chunk, 2, 4)
        else:
            own_rows(chunk)
            finish(chunk)
        if chunk == 1:
            hand_over()
        if chunk == FAR_AFTER:
            far_rows()
            finish(0)

    for i in range(NCH):
        wait_all(o_recv, o_rs, Q_PARTS[i], i)

    pltpu.make_async_copy(arrived, arrived, v_ss).wait()
    for i, part in enumerate(K_PARTS):
        wait_all(k_send, k_ss, part, i)
    for i, part in enumerate(Q_PARTS):
        wait_all(q_send, q_ss, part, i)
        wait_all(o_send, o_ss, part, i)

    for first, here, bufs in (
        (2, near_chip, (kx3.at[0], vx3.at[0])),
        (6, jnp.logical_not(near_chip), (kx3.at[0], vx3.at[0])),
        (4, far_chip, (kx4.at[0], vx4.at[0])),
        (8, jnp.logical_not(far_chip), (kx4.at[0], vx4.at[0])),
    ):

        @pl.when(here)
        def _(first=first, bufs=bufs):
            for i, buf in enumerate(bufs):
                hop(buf, buf, first + i, partner).wait_send()

    @pl.when(seq % 2 == 0)
    def _():
        hop(kx2, kx2, 0, seq).wait_send()
        hop(vx2, vx2, 1, seq).wait_send()


def unsort_kernel(o_ref, out_hbm, stage, sems):
    rows = iota((BLK, BLK), 0)
    perm = (iota((BLK, BLK), 1) == ((rows & 15) << 4) + (rows >> 4)).astype(jnp.bfloat16)
    copies = []
    for j in range(0, NB, 2):
        cols = []
        for h in (j, j + 1):
            groups = [SHIFTS.index((r - h) % 16) for r in range(16)]
            cols.append(
                jnp.concatenate([o_ref[h, g * 16 : (g + 1) * 16] for g in groups], axis=0)
            )
        stage[:, j * HD : (j + 2) * HD] = jnp.dot(
            perm, jnp.concatenate(cols, axis=1), preferred_element_type=jnp.float32
        ).astype(jnp.bfloat16)
        if j % 4 == 2:
            here = (slice(None), pl.ds((j - 2) * HD, 4 * HD))
            copy = pltpu.make_async_copy(stage.at[here], out_hbm.at[here], sems.at[j // 4])
            copy.start()
            copies.append(copy)
    for copy in copies:
        copy.wait()


def shards(queries, keys, values):
    bf, f32 = jnp.bfloat16, jnp.float32
    vm = pltpu.VMEM
    blocks = vm((NB, BLK, HD), bf)
    dma = pltpu.SemaphoreType.DMA
    nk = len(K_PARTS)
    queries, keys, values = (
        pltpu.with_memory_space_constraint(x, pltpu.HBM) for x in (queries, keys, values)
    )
    sorted_out = pl.pallas_call(
        kernel,
        out_shape=pltpu.VMEM((NB, BLK, HD), bf),
        in_specs=[pl.BlockSpec(memory_space=pltpu.HBM)] * 3,
        out_specs=pl.BlockSpec(memory_space=pltpu.VMEM),
        scratch_shapes=[
            vm((2, BLK, NB * HD), bf),
            *[blocks] * 7,
            vm((NB, 64, HD), bf), vm((NB, 64, HD), bf),
            vm((2, NB, 32, HD), bf), vm((2, NB, 32, HD), bf),
            vm((2, 2, NB, 16, HD), bf), vm((2, 2, NB, 16, HD), bf),
            *[vm((2, NB, CH, HD), f32)] * 3,
            vm((BLK, BLK), bf), vm((BLK, BLK), bf), vm((BLK, BLK), f32),
            vm((128, 128), f32), vm((64, 128), f32), vm((64, 128), f32), vm((32, 128), f32),
            dma((2,)), dma, dma((NCH,)), dma((nk,)), dma, dma((NCH,)),
            dma((NCH,)), dma((nk,)), dma, dma((NCH,)), dma((10,)), dma((10,)),
        ],
        compiler_params=pltpu.CompilerParams(
            collective_id=0, has_side_effects=True, vmem_limit_bytes=48 * 2**20
        ),
    )(queries, keys, values)
    sorted_out = pltpu.with_memory_space_constraint(sorted_out, pltpu.VMEM)
    return pl.pallas_call(
        unsort_kernel,
        out_shape=jax.ShapeDtypeStruct((BLK, NB * HD), bf),
        in_specs=[pl.BlockSpec(memory_space=pltpu.VMEM)],
        out_specs=pl.BlockSpec(memory_space=pl.ANY),
        scratch_shapes=[vm((BLK, NB * HD), bf), dma((4,))],
        compiler_params=pltpu.CompilerParams(vmem_limit_bytes=16 * 2**20),
    )(sorted_out)


def solution(mesh):
    spec = P(("seq", "head"), None)
    return jax.shard_map(
        shards, mesh=mesh, in_specs=(spec, spec, spec), out_specs=spec, check_vma=False
    )
```
